32 devices in a mesh: ctx: 8 (over z, x), head: 4 (over y, core).
Axes of the slice: x: 2, y: 2, z: 4, core: 2. Of those that a mesh axis runs over, the one named last changes fastest.
Arguments:
- queries: bfloat16 [2048, 4096], P('ctx', 'head')
- keys: bfloat16 [2048, 1024], P('ctx', 'head')
- values: bfloat16 [2048, 1024], P('ctx', 'head'), may hold values from -6 to 6
- lengths: int32 [8], replicated, may hold values from 1 to 1024, 2048 in all
- out_weight: bfloat16 [4096, 4096], P('head'), may hold values from -0.375 to 0.375
Outputs:
- projected: bfloat16 [2048, 4096], P(('ctx', 'head'))
The draws below stay inside these ranges and needn't reach their ends.
Inputs may be any that keep to these rules, and one draw needn't show every extreme that they name: The lengths sum to 2048; the longest document has exactly 1024 tokens.
All inputs are finite; a program needn't handle non-finite values.
Results may differ from the reference program's by a relative error of at most 0.015.
Values may be sent and summed in bfloat16 or wider, within the bound.
A program may use at most 64 MiB of HBM per device.

```python
import math
import jax
import jax.numpy as jnp
import numpy as np
from jax import lax

D = 4096
QUERY_HEADS = 32
KEY_VALUE_HEADS = 8
HEAD_SIZE = 128
TOKENS_PER_INDEX = 256
PACKED_TOKENS = 2048
DOCUMENT_SPAN = 4
MAXDOC = 1024
NDOCS = 8
N_HEAD = 4


def joint_draw(key):
    query_key = jax.random.fold_in(key, 11)
    key_random_seed = jax.random.fold_in(key, 12)
    starting_keys = jax.random.normal(key_random_seed, (PACKED_TOKENS, KEY_VALUE_HEADS * HEAD_SIZE), jnp.float32)
    base_queries = jax.random.normal(query_key, (PACKED_TOKENS, QUERY_HEADS * HEAD_SIZE), jnp.float32)
    return (base_queries, starting_keys)


def draw_queries(key, part):
    return joint_draw(key)[0].astype(jnp.bfloat16)


def draw_keys(key, part):
    return joint_draw(key)[1].astype(jnp.bfloat16)


def block_scale(key, dims, shards, least, largest):
    loudness, own = 1.0, jax.random.fold_in(key, 6)
    for dim, blocks in shards:
        heights = jnp.exp(jax.random.uniform(jax.random.fold_in(own, dim), (blocks,), jnp.float32, least / len(shards), largest / len(shards)))
        loudness = loudness * jnp.repeat(heights, dims[dim] // blocks).reshape([-1 if axis == dim else 1 for axis in range(len(dims))])
    return loudness


def split_up(number_of, total, reach, skew):
    weights = [(1 << 20) // math.isqrt(rank ** skew) + 1 for rank in range(2, number_of + 1)]
    surplus, holding = total - reach - (number_of - 1), [1] * (number_of - 1)
    while surplus > 0:
        free = [i for i in range(number_of - 1) if holding[i] < reach]
        whole, left = sum([weights[i] for i in free]), surplus
        for i in free:
            more = min(reach - holding[i], max(1, left * weights[i] // whole), surplus)
            holding[i] = holding[i] + more
            surplus = surplus - more
    return np.array([reach] + holding)


def uneven(key, number_of, total, reach, lean):
    if number_of == 2:
        one = jax.random.randint(key, (), max(1, total - reach), min(reach, total - 1) + 1)
        return jnp.stack([one, total - one])
    sizes = jnp.asarray(split_up(number_of, total, reach, lean), jnp.int32)
    twos = (number_of - 1) // 2
    giver, sink = sizes[1:1 + 2 * twos:2], sizes[2:2 + 2 * twos:2]
    margin = jnp.minimum(giver - 1, reach - sink)
    shifted = jax.random.randint(jax.random.fold_in(key, 1), (twos,), 0, 1 << 20) % (margin + 1)
    sizes = sizes.at[1:1 + 2 * twos:2].set(giver - shifted).at[2:2 + 2 * twos:2].set(sink + shifted)
    return sizes[jax.random.permutation(jax.random.fold_in(key, 2), number_of)]


def scatter_about(own_key, shape, width, bound, shards=(), kind=jnp.bfloat16):
    drawn = jax.random.normal(own_key, shape, jnp.float32) * width
    if len(shards) > 0:
        drawn = block_scale(own_key, shape, shards, -0.22, 0.18) * drawn
    return jnp.clip(drawn, min=-bound, max=bound).astype(kind)


def setup_inputs(seed: int = 0) -> dict:
    key_of = jax.random.split(jax.random.key(seed), 6)
    queries = draw_queries(jax.random.fold_in(key_of[5], 71), 0)
    keys = draw_keys(jax.random.fold_in(key_of[5], 71), 0)
    values = scatter_about(key_of[2], (PACKED_TOKENS, KEY_VALUE_HEADS * HEAD_SIZE), 1.0, 6.0, ((0, 8), (1, 4)))
    lengths = uneven(key_of[3], NDOCS, PACKED_TOKENS, MAXDOC, 2).astype(jnp.int32)
    out_weight = scatter_about(key_of[4], (D, D), 256 ** -0.5, 0.375, ((0, 4),))
    return {"queries": queries, "keys": keys, "values": values, "lengths": lengths, "out_weight": out_weight}


def doc_of(positions, ends):
    return jnp.sum((positions[:, None] >= ends[None, :]).astype(jnp.int32), axis=1).astype(jnp.int32)


def reference(queries, keys, values, lengths, out_weight):
    ends = jnp.cumsum(lengths).astype(jnp.int32)
    query_group = QUERY_HEADS // KEY_VALUE_HEADS
    block_width = (DOCUMENT_SPAN + 1) * TOKENS_PER_INDEX
    padding_rows = jnp.zeros((DOCUMENT_SPAN * TOKENS_PER_INDEX, KEY_VALUE_HEADS * HEAD_SIZE), keys.dtype)
    padded_keys = jnp.concatenate([padding_rows, keys], axis=0)
    padded_values = jnp.concatenate([padding_rows, values], axis=0)
    score_scale = 1.0 / (HEAD_SIZE ** 0.5)

    def block(index):
        first_index = (index * TOKENS_PER_INDEX).astype(jnp.int32)
        query_block = lax.dynamic_slice_in_dim(queries, first_index, TOKENS_PER_INDEX, 0).reshape(TOKENS_PER_INDEX, KEY_VALUE_HEADS, query_group, HEAD_SIZE)
        key_block = lax.dynamic_slice_in_dim(padded_keys, first_index, block_width, 0).reshape(block_width, KEY_VALUE_HEADS, HEAD_SIZE)
        value_block = lax.dynamic_slice_in_dim(padded_values, first_index, block_width, 0).reshape(block_width, KEY_VALUE_HEADS, HEAD_SIZE)
        qpos = first_index + jnp.arange(TOKENS_PER_INDEX, dtype=jnp.int32)
        kpos = first_index - DOCUMENT_SPAN * TOKENS_PER_INDEX + jnp.arange(block_width, dtype=jnp.int32)
        allowed = (doc_of(kpos, ends)[None, :] == doc_of(qpos, ends)[:, None]) & (kpos[None, :] <= qpos[:, None]) & (kpos[None, :] >= 0)
        logit_scores = jnp.einsum('hqnp,zqp->qnhz', query_block.astype(jnp.float32), key_block.astype(jnp.float32)) * score_scale
        logit_scores = jnp.where(allowed, logit_scores, jnp.float32(-1e30))
        top = jnp.max(logit_scores, axis=-1, keepdims=True)
        weights = jnp.where(allowed, jnp.exp(logit_scores - top), jnp.float32(0.0))
        total = jnp.sum(weights, axis=-1)
        rounded_length = weights.astype(jnp.bfloat16)
        summed_output = jnp.einsum('wcju,uwn->wcjn', rounded_length.astype(jnp.float32), value_block.astype(jnp.float32))
        result = summed_output / total[..., None]
        return jnp.transpose(result, (2, 0, 1, 3)).reshape(TOKENS_PER_INDEX, QUERY_HEADS * HEAD_SIZE).astype(jnp.bfloat16)

    blocks = PACKED_TOKENS // TOKENS_PER_INDEX
    attended = lax.map(block, jnp.arange(blocks, dtype=jnp.int32)).reshape(PACKED_TOKENS, D)
    groups = N_HEAD
    group_width = D // N_HEAD
    weight_groups = out_weight.reshape(groups, group_width, D).astype(jnp.float32)

    def project(index):
        first_index = (index * TOKENS_PER_INDEX).astype(jnp.int32)
        rows = lax.dynamic_slice_in_dim(attended, first_index, TOKENS_PER_INDEX, 0).reshape(TOKENS_PER_INDEX, groups, group_width)
        partial_value = jnp.einsum('tgk,gkn->gtn', rows.astype(jnp.float32), weight_groups)
        partial_value = partial_value.astype(jnp.bfloat16).astype(jnp.float32)
        return jnp.sum(partial_value, axis=0).astype(jnp.bfloat16)

    return lax.map(project, jnp.arange(blocks, dtype=jnp.int32)).reshape(PACKED_TOKENS, D)
```

```python
import math

import jax
import jax.numpy as jnp
from jax import lax
from jax.experimental import pallas as pl
from jax.experimental.pallas import tpu as pltpu
from jax.sharding import PartitionSpec as P

HEAD_SIZE = 128
MESH = pl.DeviceIdType.MESH
MASKED = -1.2e31
CHUNK = 512


def fused_kernel(
    lengths, queries, keys, values, weight, out,
    q_vm, kv_own, window, w_vm, q_t, top, total, accum, att,
    near_send, near_recv, far_send, far_recv, pair_send, pair_recv, far_keep, own_keep,
    load_sem, w_sem, up_send, up_recv, side_send, side_recv, core_send, core_recv, y_send, y_recv,
):
    tok = q_vm.shape[0]
    local_kv = kv_own.shape[1]
    heads = q_t.shape[0]
    group = heads // local_kv
    chunks = w_vm.shape[0]
    rows = tok // 4
    scale = math.log2(math.e) / math.sqrt(HEAD_SIZE)

    ctx = lax.axis_index("ctx")
    head = lax.axis_index("head")
    z, x = ctx // 2, ctx % 2
    y, core = head // 2, head % 2
    last = lax.axis_size("ctx") // 2 - 1
    side = 2 * z + 1 - x
    core_nbr = 2 * y + 1 - core
    y_nbr = 2 * (1 - y) + core

    loads = [pltpu.make_async_copy(queries, q_vm, load_sem.at[0])]
    for h in range(local_kv):
        lanes = pl.ds(h * HEAD_SIZE, HEAD_SIZE)
        loads.append(pltpu.make_async_copy(keys.at[:, lanes], kv_own.at[0, h], load_sem.at[1 + 2 * h]))
        loads.append(pltpu.make_async_copy(values.at[:, lanes], kv_own.at[1, h], load_sem.at[2 + 2 * h]))
    for load in loads:
        load.start()

    barrier = pltpu.get_barrier_semaphore()

    def greet(c, h):
        pl.semaphore_signal(barrier, inc=1, device_id=(c, h), device_id_type=MESH)

    greet(side, head)
    greet(ctx, core_nbr)
    greet(ctx, y_nbr)

    @pl.when(z > 0)
    def _():
        greet(ctx - 2, head)

    @pl.when(z < last)
    def _():
        greet(ctx + 2, head)

    pl.semaphore_wait(barrier, 3 + jnp.minimum(z, 1) + jnp.minimum(last - z, 1))

    def remote(src, dst, send, recv, c, h):
        return pltpu.make_async_remote_copy(
            src_ref=src, dst_ref=dst, send_sem=send, recv_sem=recv, device_id=(c, h), device_id_type=MESH
        )

    def own(t, h):
        source = keys if t == 0 else values
        return source.at[:, pl.ds(h * HEAD_SIZE, HEAD_SIZE)]

    def up(which, t, h):
        src = own(t, h) if which == 0 else window.at[1, t, h]
        return remote(src, window.at[1 + 2 * which, t, h], up_send.at[which, t, h], up_recv.at[which, t, h], ctx + 2, head)

    def side_from(src, which, t, h):
        return remote(src, window.at[2 * which, t, h], side_send.at[which, t, h], side_recv.at[which, t, h], side, head)

    for h in range(local_kv):
        for t in range(2):
            @pl.when(z < last)
            def _():
                up(0, t, h).start()

            @pl.when(x == 0)
            def _():
                side_from(own(t, h), 0, t, h).start()

    w_loads = [
        pltpu.make_async_copy(weight.at[:, pl.ds(c * CHUNK, CHUNK)], w_vm.at[c], w_sem.at[c]) for c in range(chunks)
    ]
    for load in w_loads:
        load.start()

    query_pos = ctx * tok + lax.broadcasted_iota(jnp.int32, (1, tok), 1)
    begin = jnp.zeros((1, tok), jnp.int32)
    end = jnp.int32(0)
    for n in range(lengths.shape[0]):
        end = end + lengths[n]
        begin = jnp.where(query_pos >= end, end, begin)
    key_row = lax.broadcasted_iota(jnp.int32, (tok, tok), 0)

    for load in loads:
        load.wait()
    for n in range(heads):
        q_t[n] = q_vm[:, n * HEAD_SIZE : (n + 1) * HEAD_SIZE].T

    def attend(h, distance):
        ref = kv_own if distance == 0 else window.at[distance - 1]
        key = ref[0, h]
        value_t = ref[1, h].T
        key_pos = key_row + (ctx - distance) * tok
        allowed = key_pos >= begin
        if distance == 0:
            allowed = allowed & (key_pos <= query_pos)
        for j in range(group):
            n = h * group + j
            s = jnp.dot(key, q_t[n], preferred_element_type=jnp.float32)
            s = jnp.where(allowed, s, jnp.float32(MASKED))
            newest = jnp.max(s, axis=0, keepdims=True)
            if distance:
                before = top[n]
                newest = jnp.maximum(before, newest)
                factor = jnp.exp2((before - newest) * scale)
            weights = jnp.exp2((s - newest) * scale)
            added = jnp.sum(weights, axis=0, keepdims=True)
            product = jnp.dot(value_t, weights.astype(jnp.bfloat16), preferred_element_type=jnp.float32)
            if distance:
                added = total[n] * factor + added
                product = accum[n] * factor + product
            top[n] = newest
            total[n] = added
            accum[n] = product

    def attend_if(h, distance):
        @pl.when(ctx >= distance)
        def _():
            attend(h, distance)

    def relay(which, h):
        @pl.when(z > which)
        def _():
            for t in range(2):
                up(which, t, h).wait_recv()
                if which == 0:
                    @pl.when(z < last)
                    def _():
                        up(1, t, h).start()

                    @pl.when(x == 0)
                    def _():
                        side_from(window.at[1, t, h], 1, t, h).start()

                    @pl.when(x == 1)
                    def _():
                        side_from(window.at[1, t, h], 0, t, h).start()
                else:
                    @pl.when(x == 1)
                    def _():
                        side_from(window.at[3, t, h], 1, t, h).start()

    def side_arrived(which, h):
        @pl.when(ctx >= 1 + 2 * which)
        def _():
            for t in range(2):
                side_from(own(t, h), which, t, h).wait_recv()

    attend(0, 0)
    relay(0, 0)
    attend(1, 0)
    attend_if(0, 2)
    relay(0, 1)
    attend_if(1, 2)
    side_arrived(0, 0)
    attend_if(0, 1)
    relay(1, 0)
    side_arrived(0, 1)
    attend_if(1, 1)
    attend_if(0, 4)
    relay(1, 1)
    attend_if(1, 4)
    side_arrived(1, 0)
    attend_if(0, 3)
    side_arrived(1, 1)
    attend_if(1, 3)

    for n in range(heads):
        ready = (accum[n] / total[n]).T.astype(jnp.bfloat16)
        for g in range(4):
            place = ((g // 2 + y) % 2) * 2 + (g % 2 + core) % 2
            att[pl.ds(pl.multiple_of(place * rows, rows), rows), n * HEAD_SIZE : (n + 1) * HEAD_SIZE] = ready[
                g * rows : (g + 1) * rows
            ]

    def far(c):
        return remote(far_send.at[c], far_recv.at[c], core_send.at[0, c], core_recv.at[0, c], ctx, core_nbr)

    def near(c):
        return remote(near_send.at[c], near_recv.at[c], core_send.at[1, c], core_recv.at[1, c], ctx, core_nbr)

    def across(c):
        return remote(pair_send.at[c], pair_recv.at[c], y_send.at[c], y_recv.at[c], ctx, y_nbr)

    def project(c):
        w_loads[c].wait()
        partial = jnp.dot(att[...], w_vm[c], preferred_element_type=jnp.float32)
        far_send[c] = partial[3 * rows :].astype(jnp.bfloat16)
        far(c).start()
        far_keep[c] = partial[2 * rows : 3 * rows]
        near_send[c] = partial[rows : 2 * rows].astype(jnp.bfloat16)
        near(c).start()
        own_keep[c] = partial[:rows]

    def pass_on(c):
        far(c).wait_recv()
        pair_send[c] = (far_keep[c] + far_recv[c].astype(jnp.float32)).astype(jnp.bfloat16)
        across(c).start()

    for c in range(chunks):
        project(c)
        if c:
            pass_on(c - 1)
    pass_on(chunks - 1)
    for c in range(chunks):
        near(c).wait_recv()
        across(c).wait_recv()
        out[:, c * CHUNK : (c + 1) * CHUNK] = (
            own_keep[c] + near_recv[c].astype(jnp.float32) + pair_recv[c].astype(jnp.float32)
        ).astype(jnp.bfloat16)

    for h in range(local_kv):
        for t in range(2):
            @pl.when(z < last)
            def _():
                up(0, t, h).wait_send()

            @pl.when((z < last) & (z > 0))
            def _():
                up(1, t, h).wait_send()

            @pl.when((x == 0) | (z > 0))
            def _():
                side_from(own(t, h), 0, t, h).wait_send()

            @pl.when(z > x)
            def _():
                side_from(own(t, h), 1, t, h).wait_send()
    for c in range(chunks):
        far(c).wait_send()
        near(c).wait_send()
        across(c).wait_send()


def fused_shards(queries, keys, values, lengths, out_weight):
    tok = queries.shape[0]
    local_kv = keys.shape[1] // HEAD_SIZE
    heads = queries.shape[1] // HEAD_SIZE
    columns = out_weight.shape[1]
    chunks = columns // CHUNK
    rows = tok // 4
    piece = (chunks, rows, CHUNK)
    bf16, f32 = jnp.bfloat16, jnp.float32
    dma = pltpu.SemaphoreType.DMA
    return pl.pallas_call(
        fused_kernel,
        out_shape=jax.ShapeDtypeStruct((rows, columns), bf16),
        in_specs=[pl.BlockSpec(memory_space=pltpu.SMEM)] + [pl.BlockSpec(memory_space=pl.ANY)] * 4,
        out_specs=pl.BlockSpec(memory_space=pltpu.VMEM),
        scratch_shapes=[
            pltpu.VMEM(queries.shape, bf16),
            pltpu.VMEM((2, local_kv, tok, HEAD_SIZE), bf16),
            pltpu.VMEM((4, 2, local_kv, tok, HEAD_SIZE), bf16),
            pltpu.VMEM((chunks, out_weight.shape[0], CHUNK), bf16),
            pltpu.VMEM((heads, HEAD_SIZE, tok), bf16),
            pltpu.VMEM((heads, 1, tok), f32),
            pltpu.VMEM((heads, 1, tok), f32),
            pltpu.VMEM((heads, HEAD_SIZE, tok), f32),
            pltpu.VMEM((tok, heads * HEAD_SIZE), bf16),
        ]
        + [pltpu.VMEM(piece, bf16)] * 6
        + [pltpu.VMEM(piece, f32)] * 2
        + [dma((1 + 2 * local_kv,)), dma((chunks,))]
        + [dma((2, 2, local_kv))] * 4
        + [dma((2, chunks))] * 2
        + [dma((chunks,))] * 2,
        compiler_params=pltpu.CompilerParams(
            collective_id=0, has_side_effects=True, vmem_limit_bytes=60 * 1024 * 1024
        ),
    )(lengths, queries, keys, values, out_weight)


def shifted(value, axis, steps):
    count = lax.axis_size(axis)
    first, last = (max(0, -steps), min(count, count - steps))
    return lax.ppermute(value, axis, [(source, source + steps) for source in range(first, last)])


def doc_of(positions, ends):
    return jnp.sum((positions[:, None] >= ends[None, :]).astype(jnp.int32), axis=1)


def shards(queries, keys, values, lengths, out_weight):
    tok = queries.shape[0]
    local_kv = keys.shape[1] // HEAD_SIZE
    query_group = queries.shape[1] // keys.shape[1]
    span = min(16, lax.axis_size("ctx") // 2)
    stretch = lax.axis_index("ctx")
    order = jnp.arange(lengths.shape[0])
    ends = jnp.sum(jnp.where(order[None, :] <= order[:, None], lengths[None, :], 0), axis=1)
    paired = jnp.stack([keys, values])
    window = paired
    have = 1
    while have < span + 1:
        count = min(have, span + 1 - have)
        received = shifted(window[:, window.shape[1] - count * tok :], "ctx", have)
        window = jnp.concatenate([received, window], axis=1)
        have = have + count
    blocks = jnp.swapaxes(window.reshape(2, span + 1, tok, local_kv * HEAD_SIZE), 0, 1)
    key_pos = (stretch - span) * tok + jnp.arange((span + 1) * tok, dtype=jnp.int32)
    key_pos = key_pos.reshape(span + 1, tok)
    query_pos = stretch * tok + jnp.arange(tok, dtype=jnp.int32)
    query_doc = doc_of(query_pos, ends)
    query_head_rows = queries.reshape(tok, local_kv, query_group, HEAD_SIZE)
    score_scale = 1.0 / HEAD_SIZE**0.5

    def step(carry, item):
        kv_block, positions = item
        allowed = (
            (doc_of(positions, ends)[None, :] == query_doc[:, None])
            & (positions[None, :] <= query_pos[:, None])
            & (positions[None, :] >= 0)
        )
        running, total, accum = carry
        key_head_rows = kv_block[0].reshape(tok, local_kv, HEAD_SIZE)
        value_heads = kv_block[1].reshape(tok, local_kv, HEAD_SIZE)
        logit_scores = (
            jnp.einsum(
                "hqnp,zqp->qnhz", query_head_rows, key_head_rows, preferred_element_type=jnp.float32
            )
            * score_scale
        )
        logit_scores = jnp.where(allowed, logit_scores, jnp.float32(-1e30))
        newest = jnp.maximum(running, jnp.max(logit_scores, axis=-1))
        factor = jnp.exp(running - newest)
        weights = jnp.where(allowed, jnp.exp(logit_scores - newest[..., None]), jnp.float32(0.0))
        total = total * factor + jnp.sum(weights, axis=-1)
        accum = accum * factor[..., None] + jnp.einsum(
            "wcju,uwn->wcjn",
            weights.astype(jnp.bfloat16),
            value_heads,
            preferred_element_type=jnp.float32,
        )
        result = (newest, total, accum)
        return (result, None)

    start_state = (
        jnp.full((local_kv, query_group, tok), -1e30, jnp.float32),
        jnp.zeros((local_kv, query_group, tok), jnp.float32),
        jnp.zeros((local_kv, query_group, tok, HEAD_SIZE), jnp.float32),
    )
    final_state, unused = lax.scan(step, start_state, (blocks, key_pos))
    attended = final_state[2] / final_state[1][..., None]
    attended = (
        jnp.transpose(attended, (2, 0, 1, 3))
        .reshape(tok, local_kv * query_group * HEAD_SIZE)
        .astype(jnp.bfloat16)
    )
    return lax.psum_scatter(
        jnp.dot(attended, out_weight, preferred_element_type=jnp.float32).astype(jnp.bfloat16),
        "head",
        scatter_dimension=0,
        tiled=True,
    )


def solution(mesh):
    in_specs = (P("ctx", "head"), P("ctx", "head"), P("ctx", "head"), P(), P("head", None))
    out_specs = P(("ctx", "head"), None)
    body = fused_shards if (mesh.shape["ctx"], mesh.shape["head"]) == (8, 4) else shards
    return jax.shard_map(body, mesh=mesh, in_specs=in_specs, out_specs=out_specs, check_vma=False)
```

```python
import math

import jax
import jax.numpy as jnp
from jax import lax
from jax.experimental import pallas as pl
from jax.experimental.pallas import tpu as pltpu
from jax.sharding import PartitionSpec as P

HEAD_SIZE = 128
MESH = pl.DeviceIdType.MESH
MASKED = -1.2e31
CHUNK = 512


def fused_kernel(
    lengths, queries, keys, values, weight, out,
    q_vm, kv_own, window, w_vm, q_t, top, total, accum, att,
    near_send, near_recv, far_send, far_recv, pair_send, pair_recv, far_keep, own_keep,
    load_sem, w_sem, up_send, up_recv, side_send, side_recv, core_send, core_recv, y_send, y_recv,
):
    tok = q_vm.shape[0]
    local_kv = kv_own.shape[1]
    heads = q_t.shape[0]
    group = heads // local_kv
    chunks = w_vm.shape[0]
    rows = tok // 4
    scale = math.log2(math.e) / math.sqrt(HEAD_SIZE)

    ctx = lax.axis_index("ctx")
    head = lax.axis_index("head")
    z, x = ctx // 2, ctx % 2
    y, core = head // 2, head % 2
    last = lax.axis_size("ctx") // 2 - 1
    side = 2 * z + 1 - x
    core_nbr = 2 * y + 1 - core
    y_nbr = 2 * (1 - y) + core

    loads = [pltpu.make_async_copy(queries, q_vm, load_sem.at[0])]
    for h in range(local_kv):
        lanes = pl.ds(h * HEAD_SIZE, HEAD_SIZE)
        loads.append(pltpu.make_async_copy(keys.at[:, lanes], kv_own.at[0, h], load_sem.at[1 + 2 * h]))
        loads.append(pltpu.make_async_copy(values.at[:, lanes], kv_own.at[1, h], load_sem.at[2 + 2 * h]))
    for load in loads:
        load.start()

    barrier = pltpu.get_barrier_semaphore()

    def greet(c, h):
        pl.semaphore_signal(barrier, inc=1, device_id=(c, h), device_id_type=MESH)

    greet(side, head)
    greet(ctx, core_nbr)
    greet(ctx, y_nbr)

    @pl.when(z > 0)
    def _():
        greet(ctx - 2, head)

    @pl.when(z < last)
    def _():
        greet(ctx + 2, head)

    pl.semaphore_wait(barrier, 3 + jnp.minimum(z, 1) + jnp.minimum(last - z, 1))

    def remote(src, dst, send, recv, c, h):
        return pltpu.make_async_remote_copy(
            src_ref=src, dst_ref=dst, send_sem=send, recv_sem=recv, device_id=(c, h), device_id_type=MESH
        )

    def own(t, h):
        source = keys if t == 0 else values
        return source.at[:, pl.ds(h * HEAD_SIZE, HEAD_SIZE)]

    def up(which, t, h):
        src = own(t, h) if which == 0 else window.at[1, t, h]
        return remote(src, window.at[1 + 2 * which, t, h], up_send.at[which, t, h], up_recv.at[which, t, h], ctx + 2, head)

    def side_from(src, which, t, h):
        return remote(src, window.at[2 * which, t, h], side_send.at[which, t, h], side_recv.at[which, t, h], side, head)

    for h in range(local_kv):
        for t in range(2):
            @pl.when(z < last)
            def _():
                up(0, t, h).start()

            @pl.when(x == 0)
            def _():
                side_from(own(t, h), 0, t, h).start()

    w_loads = [
        pltpu.make_async_copy(weight.at[:, pl.ds(c * CHUNK, CHUNK)], w_vm.at[c], w_sem.at[c]) for c in range(chunks)
    ]
    for load in w_loads:
        load.start()

    query_pos = ctx * tok + lax.broadcasted_iota(jnp.int32, (1, tok), 1)
    begin = jnp.zeros((1, tok), jnp.int32)
    end = jnp.int32(0)
    for n in range(lengths.shape[0]):
        end = end + lengths[n]
        begin = jnp.where(query_pos >= end, end, begin)
    key_row = lax.broadcasted_iota(jnp.int32, (tok, tok), 0)

    for load in loads:
        load.wait()
    for n in range(heads):
        q_t[n] = q_vm[:, n * HEAD_SIZE : (n + 1) * HEAD_SIZE].T

    def attend(h, distance):
        ref = kv_own if distance == 0 else window.at[distance - 1]
        key = ref[0, h]
        value_t = ref[1, h].T
        key_pos = key_row + (ctx - distance) * tok
        allowed = key_pos >= begin
        if distance == 0:
            allowed = allowed & (key_pos <= query_pos)
        tiles = [(h * group + j, pl.ds(i * 128, 128), i) for j in range(group) for i in range(tok // 128)]

        def scores(tile):
            return jnp.dot(key, q_t[tile[0], :, tile[1]], preferred_element_type=jnp.float32)

        masks = [allowed[:, i * 128 : (i + 1) * 128] for i in range(tok // 128)]
        queue = [scores(tile) for tile in tiles[:4]]
        for place, (n, lanes, i) in enumerate(tiles):
            if place + 4 < len(tiles):
                queue.append(scores(tiles[place + 4]))
            s = jnp.where(masks[i], queue[place], jnp.float32(MASKED))
            newest = jnp.max(s, axis=0, keepdims=True)
            if distance:
                before = top[n, :, lanes]
                newest = jnp.maximum(before, newest)
                factor = jnp.exp2((before - newest) * scale)
            weights = jnp.exp2((s - newest) * scale)
            added = jnp.sum(weights, axis=0, keepdims=True)
            product = jnp.dot(value_t, weights.astype(jnp.bfloat16), preferred_element_type=jnp.float32)
            if distance:
                added = total[n, :, lanes] * factor + added
                product = accum[n, :, lanes] * factor + product
            top[n, :, lanes] = newest
            total[n, :, lanes] = added
            accum[n, :, lanes] = product

    def attend_if(h, distance):
        @pl.when(ctx >= distance)
        def _():
            attend(h, distance)

    def relay(which, h):
        @pl.when(z > which)
        def _():
            for t in range(2):
                up(which, t, h).wait_recv()
                if which == 0:
                    @pl.when(z < last)
                    def _():
                        up(1, t, h).start()

                    @pl.when(x == 0)
                    def _():
                        side_from(window.at[1, t, h], 1, t, h).start()

                    @pl.when(x == 1)
                    def _():
                        side_from(window.at[1, t, h], 0, t, h).start()
                else:
                    @pl.when(x == 1)
                    def _():
                        side_from(window.at[3, t, h], 1, t, h).start()

    def side_arrived(which, h):
        @pl.when(ctx >= 1 + 2 * which)
        def _():
            for t in range(2):
                side_from(own(t, h), which, t, h).wait_recv()

    def finish(h):
        for n in range(h * group, (h + 1) * group):
            ready = (accum[n] / total[n]).T.astype(jnp.bfloat16)
            for g in range(4):
                place = ((g // 2 + y) % 2) * 2 + (g % 2 + core) % 2
                att[pl.ds(pl.multiple_of(place * rows, rows), rows), n * HEAD_SIZE : (n + 1) * HEAD_SIZE] = ready[
                    g * rows : (g + 1) * rows
                ]

    attend(0, 0)
    relay(0, 0)
    attend(1, 0)
    attend_if(0, 2)
    relay(0, 1)
    attend_if(1, 2)
    side_arrived(0, 0)
    attend_if(0, 1)
    relay(1, 0)
    side_arrived(0, 1)
    attend_if(1, 1)
    attend_if(0, 4)
    relay(1, 1)
    attend_if(1, 4)
    side_arrived(1, 0)
    attend_if(0, 3)
    finish(0)
    side_arrived(1, 1)
    attend_if(1, 3)
    finish(1)

    def far(c):
        return remote(far_send.at[c], far_recv.at[c], core_send.at[0, c], core_recv.at[0, c], ctx, core_nbr)

    def near(c):
        return remote(near_send.at[c], near_recv.at[c], core_send.at[1, c], core_recv.at[1, c], ctx, core_nbr)

    def across(c):
        return remote(pair_send.at[c], pair_recv.at[c], y_send.at[c], y_recv.at[c], ctx, y_nbr)

    def project(c):
        w_loads[c].wait()
        partial = jnp.dot(att[...], w_vm[c], preferred_element_type=jnp.float32)
        far_send[c] = partial[3 * rows :].astype(jnp.bfloat16)
        far(c).start()
        far_keep[c] = partial[2 * rows : 3 * rows]
        near_send[c] = partial[rows : 2 * rows].astype(jnp.bfloat16)
        near(c).start()
        own_keep[c] = partial[:rows]

    def pass_on(c):
        far(c).wait_recv()
        pair_send[c] = (far_keep[c] + far_recv[c].astype(jnp.float32)).astype(jnp.bfloat16)
        across(c).start()

    for c in range(chunks):
        project(c)
        if c:
            pass_on(c - 1)
    pass_on(chunks - 1)
    for c in range(chunks):
        near(c).wait_recv()
        across(c).wait_recv()
        out[:, c * CHUNK : (c + 1) * CHUNK] = (
            own_keep[c] + near_recv[c].astype(jnp.float32) + pair_recv[c].astype(jnp.float32)
        ).astype(jnp.bfloat16)

    for h in range(local_kv):
        for t in range(2):
            @pl.when(z < last)
            def _():
                up(0, t, h).wait_send()

            @pl.when((z < last) & (z > 0))
            def _():
                up(1, t, h).wait_send()

            @pl.when((x == 0) | (z > 0))
            def _():
                side_from(own(t, h), 0, t, h).wait_send()

            @pl.when(z > x)
            def _():
                side_from(own(t, h), 1, t, h).wait_send()
    for c in range(chunks):
        far(c).wait_send()
        near(c).wait_send()
        across(c).wait_send()


def fused_shards(queries, keys, values, lengths, out_weight):
    tok = queries.shape[0]
    local_kv = keys.shape[1] // HEAD_SIZE
    heads = queries.shape[1] // HEAD_SIZE
    columns = out_weight.shape[1]
    chunks = columns // CHUNK
    rows = tok // 4
    piece = (chunks, rows, CHUNK)
    bf16, f32 = jnp.bfloat16, jnp.float32
    dma = pltpu.SemaphoreType.DMA
    return pl.pallas_call(
        fused_kernel,
        out_shape=jax.ShapeDtypeStruct((rows, columns), bf16),
        in_specs=[pl.BlockSpec(memory_space=pltpu.SMEM)] + [pl.BlockSpec(memory_space=pl.ANY)] * 4,
        out_specs=pl.BlockSpec(memory_space=pltpu.VMEM),
        scratch_shapes=[
            pltpu.VMEM(queries.shape, bf16),
            pltpu.VMEM((2, local_kv, tok, HEAD_SIZE), bf16),
            pltpu.VMEM((4, 2, local_kv, tok, HEAD_SIZE), bf16),
            pltpu.VMEM((chunks, out_weight.shape[0], CHUNK), bf16),
            pltpu.VMEM((heads, HEAD_SIZE, tok), bf16),
            pltpu.VMEM((heads, 1, tok), f32),
            pltpu.VMEM((heads, 1, tok), f32),
            pltpu.VMEM((heads, HEAD_SIZE, tok), f32),
            pltpu.VMEM((tok, heads * HEAD_SIZE), bf16),
        ]
        + [pltpu.VMEM(piece, bf16)] * 6
        + [pltpu.VMEM(piece, f32)] * 2
        + [dma((1 + 2 * local_kv,)), dma((chunks,))]
        + [dma((2, 2, local_kv))] * 4
        + [dma((2, chunks))] * 2
        + [dma((chunks,))] * 2,
        compiler_params=pltpu.CompilerParams(
            collective_id=0, has_side_effects=True, vmem_limit_bytes=60 * 1024 * 1024
        ),
    )(lengths, queries, keys, values, out_weight)


def shifted(value, axis, steps):
    count = lax.axis_size(axis)
    first, last = (max(0, -steps), min(count, count - steps))
    return lax.ppermute(value, axis, [(source, source + steps) for source in range(first, last)])


def doc_of(positions, ends):
    return jnp.sum((positions[:, None] >= ends[None, :]).astype(jnp.int32), axis=1)


def shards(queries, keys, values, lengths, out_weight):
    tok = queries.shape[0]
    local_kv = keys.shape[1] // HEAD_SIZE
    query_group = queries.shape[1] // keys.shape[1]
    span = min(16, lax.axis_size("ctx") // 2)
    stretch = lax.axis_index("ctx")
    order = jnp.arange(lengths.shape[0])
    ends = jnp.sum(jnp.where(order[None, :] <= order[:, None], lengths[None, :], 0), axis=1)
    paired = jnp.stack([keys, values])
    window = paired
    have = 1
    while have < span + 1:
        count = min(have, span + 1 - have)
        received = shifted(window[:, window.shape[1] - count * tok :], "ctx", have)
        window = jnp.concatenate([received, window], axis=1)
        have = have + count
    blocks = jnp.swapaxes(window.reshape(2, span + 1, tok, local_kv * HEAD_SIZE), 0, 1)
    key_pos = (stretch - span) * tok + jnp.arange((span + 1) * tok, dtype=jnp.int32)
    key_pos = key_pos.reshape(span + 1, tok)
    query_pos = stretch * tok + jnp.arange(tok, dtype=jnp.int32)
    query_doc = doc_of(query_pos, ends)
    query_head_rows = queries.reshape(tok, local_kv, query_group, HEAD_SIZE)
    score_scale = 1.0 / HEAD_SIZE**0.5

    def step(carry, item):
        kv_block, positions = item
        allowed = (
            (doc_of(positions, ends)[None, :] == query_doc[:, None])
            & (positions[None, :] <= query_pos[:, None])
            & (positions[None, :] >= 0)
        )
        running, total, accum = carry
        key_head_rows = kv_block[0].reshape(tok, local_kv, HEAD_SIZE)
        value_heads = kv_block[1].reshape(tok, local_kv, HEAD_SIZE)
        logit_scores = (
            jnp.einsum(
                "hqnp,zqp->qnhz", query_head_rows, key_head_rows, preferred_element_type=jnp.float32
            )
            * score_scale
        )
        logit_scores = jnp.where(allowed, logit_scores, jnp.float32(-1e30))
        newest = jnp.maximum(running, jnp.max(logit_scores, axis=-1))
        factor = jnp.exp(running - newest)
        weights = jnp.where(allowed, jnp.exp(logit_scores - newest[..., None]), jnp.float32(0.0))
        total = total * factor + jnp.sum(weights, axis=-1)
        accum = accum * factor[..., None] + jnp.einsum(
            "wcju,uwn->wcjn",
            weights.astype(jnp.bfloat16),
            value_heads,
            preferred_element_type=jnp.float32,
        )
        result = (newest, total, accum)
        return (result, None)

    start_state = (
        jnp.full((local_kv, query_group, tok), -1e30, jnp.float32),
        jnp.zeros((local_kv, query_group, tok), jnp.float32),
        jnp.zeros((local_kv, query_group, tok, HEAD_SIZE), jnp.float32),
    )
    final_state, unused = lax.scan(step, start_state, (blocks, key_pos))
    attended = final_state[2] / final_state[1][..., None]
    attended = (
        jnp.transpose(attended, (2, 0, 1, 3))
        .reshape(tok, local_kv * query_group * HEAD_SIZE)
        .astype(jnp.bfloat16)
    )
    return lax.psum_scatter(
        jnp.dot(attended, out_weight, preferred_element_type=jnp.float32).astype(jnp.bfloat16),
        "head",
        scatter_dimension=0,
        tiled=True,
    )


def solution(mesh):
    in_specs = (P("ctx", "head"), P("ctx", "head"), P("ctx", "head"), P(), P("head", None))
    out_specs = P(("ctx", "head"), None)
    body = fused_shards if (mesh.shape["ctx"], mesh.shape["head"]) == (8, 4) else shards
    return jax.shard_map(body, mesh=mesh, in_specs=in_specs, out_specs=out_specs, check_vma=False)
```

```python
import math

import jax
import jax.numpy as jnp
from jax import lax
from jax.experimental import pallas as pl
from jax.experimental.pallas import tpu as pltpu
from jax.sharding import PartitionSpec as P

HEAD_SIZE = 128
MESH = pl.DeviceIdType.MESH
MASKED = -1.2e31
CHUNK = 512


def fused_kernel(
    lengths, queries, keys, values, weight, mine, theirs,
    q_vm, kv_own, window, w_vm, q_t, top, total, accum, att,
    near_send, near_recv, far_send, far_recv, pair_send, far_keep, own_keep,
    load_sem, w_sem, up_send, up_recv, side_send, side_recv, core_send, core_recv, y_send, y_recv, mine_sem,
):
    tok = q_vm.shape[0]
    local_kv = kv_own.shape[1]
    heads = q_t.shape[0]
    group = heads // local_kv
    chunks = w_vm.shape[0]
    rows = tok // 4
    scale = math.log2(math.e) / math.sqrt(HEAD_SIZE)

    ctx = lax.axis_index("ctx")
    head = lax.axis_index("head")
    z, x = ctx // 2, ctx % 2
    y, core = head // 2, head % 2
    last = lax.axis_size("ctx") // 2 - 1
    side = 2 * z + 1 - x
    core_nbr = 2 * y + 1 - core
    y_nbr = 2 * (1 - y) + core

    loads = [pltpu.make_async_copy(queries, q_vm, load_sem.at[0])]
    for h in range(local_kv):
        lanes = pl.ds(h * HEAD_SIZE, HEAD_SIZE)
        loads.append(pltpu.make_async_copy(keys.at[:, lanes], kv_own.at[0, h], load_sem.at[1 + 2 * h]))
        loads.append(pltpu.make_async_copy(values.at[:, lanes], kv_own.at[1, h], load_sem.at[2 + 2 * h]))
    for load in loads:
        load.start()

    barrier = pltpu.get_barrier_semaphore()

    def greet(c, h):
        pl.semaphore_signal(barrier, inc=1, device_id=(c, h), device_id_type=MESH)

    greet(side, head)
    greet(ctx, core_nbr)
    greet(ctx, y_nbr)

    @pl.when(z > 0)
    def _():
        greet(ctx - 2, head)

    @pl.when(z < last)
    def _():
        greet(ctx + 2, head)

    pl.semaphore_wait(barrier, 3 + jnp.minimum(z, 1) + jnp.minimum(last - z, 1))

    def remote(src, dst, send, recv, c, h):
        return pltpu.make_async_remote_copy(
            src_ref=src, dst_ref=dst, send_sem=send, recv_sem=recv, device_id=(c, h), device_id_type=MESH
        )

    def own(t, h):
        source = keys if t == 0 else values
        return source.at[:, pl.ds(h * HEAD_SIZE, HEAD_SIZE)]

    def up(which, t, h):
        src = own(t, h) if which == 0 else window.at[1, t, h]
        return remote(src, window.at[1 + 2 * which, t, h], up_send.at[which, t, h], up_recv.at[which, t, h], ctx + 2, head)

    def side_from(src, which, t, h):
        return remote(src, window.at[2 * which, t, h], side_send.at[which, t, h], side_recv.at[which, t, h], side, head)

    for h in range(local_kv):
        for t in range(2):
            @pl.when(z < last)
            def _():
                up(0, t, h).start()

            @pl.when(x == 0)
            def _():
                side_from(own(t, h), 0, t, h).start()

    w_loads = [
        pltpu.make_async_copy(weight.at[:, pl.ds(c * CHUNK, CHUNK)], w_vm.at[c], w_sem.at[c]) for c in range(chunks)
    ]
    for load in w_loads:
        load.start()

    query_pos = ctx * tok + lax.broadcasted_iota(jnp.int32, (1, tok), 1)
    begin = jnp.zeros((1, tok), jnp.int32)
    end = jnp.int32(0)
    for n in range(lengths.shape[0]):
        end = end + lengths[n]
        begin = jnp.where(query_pos >= end, end, begin)
    key_row = lax.broadcasted_iota(jnp.int32, (tok, tok), 0)

    for load in loads:
        load.wait()
    for n in range(heads):
        q_t[n] = q_vm[:, n * HEAD_SIZE : (n + 1) * HEAD_SIZE].T

    def attend(h, distance):
        ref = kv_own if distance == 0 else window.at[distance - 1]
        key = ref[0, h]
        value_t = ref[1, h].T
        key_pos = key_row + (ctx - distance) * tok
        allowed = key_pos >= begin
        if distance == 0:
            allowed = allowed & (key_pos <= query_pos)
        tiles = [(h * group + j, pl.ds(i * 128, 128), i) for j in range(group) for i in range(tok // 128)]

        def scores(tile):
            return jnp.dot(key, q_t[tile[0], :, tile[1]], preferred_element_type=jnp.float32)

        masks = [allowed[:, i * 128 : (i + 1) * 128] for i in range(tok // 128)]
        queue = [scores(tile) for tile in tiles[:4]]
        for place, (n, lanes, i) in enumerate(tiles):
            if place + 4 < len(tiles):
                queue.append(scores(tiles[place + 4]))
            s = jnp.where(masks[i], queue[place], jnp.float32(MASKED))
            newest = jnp.max(s, axis=0, keepdims=True)
            if distance:
                before = top[n, :, lanes]
                newest = jnp.maximum(before, newest)
                factor = jnp.exp2((before - newest) * scale)
            weights = jnp.exp2((s - newest) * scale)
            added = jnp.sum(weights, axis=0, keepdims=True)
            product = jnp.dot(value_t, weights.astype(jnp.bfloat16), preferred_element_type=jnp.float32)
            if distance:
                added = total[n, :, lanes] * factor + added
                product = accum[n, :, lanes] * factor + product
            top[n, :, lanes] = newest
            total[n, :, lanes] = added
            accum[n, :, lanes] = product

    def attend_if(h, distance):
        @pl.when(ctx >= distance)
        def _():
            attend(h, distance)

    def relay(which, h):
        @pl.when(z > which)
        def _():
            for t in range(2):
                up(which, t, h).wait_recv()
                if which == 0:
                    @pl.when(z < last)
                    def _():
                        up(1, t, h).start()

                    @pl.when(x == 0)
                    def _():
                        side_from(window.at[1, t, h], 1, t, h).start()

                    @pl.when(x == 1)
                    def _():
                        side_from(window.at[1, t, h], 0, t, h).start()
                else:
                    @pl.when(x == 1)
                    def _():
                        side_from(window.at[3, t, h], 1, t, h).start()

    def side_arrived(which, h):
        @pl.when(ctx >= 1 + 2 * which)
        def _():
            for t in range(2):
                side_from(own(t, h), which, t, h).wait_recv()

    def finish(h):
        for n in range(h * group, (h + 1) * group):
            ready = (accum[n] / total[n]).T.astype(jnp.bfloat16)
            for g in range(4):
                place = ((g // 2 + y) % 2) * 2 + (g % 2 + core) % 2
                att[pl.ds(pl.multiple_of(place * rows, rows), rows), n * HEAD_SIZE : (n + 1) * HEAD_SIZE] = ready[
                    g * rows : (g + 1) * rows
                ]

    attend(0, 0)
    relay(0, 0)
    attend(1, 0)
    attend_if(0, 2)
    relay(0, 1)
    attend_if(1, 2)
    side_arrived(0, 0)
    attend_if(0, 1)
    relay(1, 0)
    side_arrived(0, 1)
    attend_if(1, 1)
    attend_if(0, 4)
    relay(1, 1)
    attend_if(1, 4)
    side_arrived(1, 0)
    attend_if(0, 3)
    finish(0)
    side_arrived(1, 1)
    attend_if(1, 3)
    finish(1)

    def far(c):
        return remote(far_send.at[c], far_recv.at[c], core_send.at[0, c], core_recv.at[0, c], ctx, core_nbr)

    def near(c):
        return remote(near_send.at[c], near_recv.at[c], core_send.at[1, c], core_recv.at[1, c], ctx, core_nbr)

    def across(c):
        return remote(pair_send.at[c], theirs.at[:, pl.ds(c * CHUNK, CHUNK)], y_send.at[c], y_recv.at[c], ctx, y_nbr)

    def project(c):
        w_loads[c].wait()
        partial = jnp.dot(att[...], w_vm[c], preferred_element_type=jnp.float32)
        far_send[c] = partial[3 * rows :].astype(jnp.bfloat16)
        far(c).start()
        far_keep[c] = partial[2 * rows : 3 * rows]
        near_send[c] = partial[rows : 2 * rows].astype(jnp.bfloat16)
        near(c).start()
        own_keep[c] = partial[:rows]

    def pass_on(c):
        far(c).wait_recv()
        pair_send[c] = (far_keep[c] + far_recv[c].astype(jnp.float32)).astype(jnp.bfloat16)
        across(c).start()

    for c in range(chunks):
        project(c)
        if c:
            pass_on(c - 1)
    pass_on(chunks - 1)
    stores = [
        pltpu.make_async_copy(own_keep.at[c], mine.at[:, pl.ds(c * CHUNK, CHUNK)], mine_sem.at[c]) for c in range(chunks)
    ]
    for c in range(chunks):
        near(c).wait_recv()
        own_keep[c] += near_recv[c].astype(jnp.float32)
        stores[c].start()
    for c in range(chunks):
        stores[c].wait()
        across(c).wait_recv()

    for h in range(local_kv):
        for t in range(2):
            @pl.when(z < last)
            def _():
                up(0, t, h).wait_send()

            @pl.when((z < last) & (z > 0))
            def _():
                up(1, t, h).wait_send()

            @pl.when((x == 0) | (z > 0))
            def _():
                side_from(own(t, h), 0, t, h).wait_send()

            @pl.when(z > x)
            def _():
                side_from(own(t, h), 1, t, h).wait_send()
    for c in range(chunks):
        far(c).wait_send()
        near(c).wait_send()
        across(c).wait_send()


def fused_shards(queries, keys, values, lengths, out_weight):
    tok = queries.shape[0]
    local_kv = keys.shape[1] // HEAD_SIZE
    heads = queries.shape[1] // HEAD_SIZE
    columns = out_weight.shape[1]
    chunks = columns // CHUNK
    rows = tok // 4
    piece = (chunks, rows, CHUNK)
    bf16, f32 = jnp.bfloat16, jnp.float32
    dma = pltpu.SemaphoreType.DMA
    mine, theirs = pl.pallas_call(
        fused_kernel,
        out_shape=[jax.ShapeDtypeStruct((rows, columns), f32), jax.ShapeDtypeStruct((rows, columns), bf16)],
        in_specs=[pl.BlockSpec(memory_space=pltpu.SMEM)] + [pl.BlockSpec(memory_space=pl.ANY)] * 4,
        out_specs=[pl.BlockSpec(memory_space=pl.ANY)] * 2,
        scratch_shapes=[
            pltpu.VMEM(queries.shape, bf16),
            pltpu.VMEM((2, local_kv, tok, HEAD_SIZE), bf16),
            pltpu.VMEM((4, 2, local_kv, tok, HEAD_SIZE), bf16),
            pltpu.VMEM((chunks, out_weight.shape[0], CHUNK), bf16),
            pltpu.VMEM((heads, HEAD_SIZE, tok), bf16),
            pltpu.VMEM((heads, 1, tok), f32),
            pltpu.VMEM((heads, 1, tok), f32),
            pltpu.VMEM((heads, HEAD_SIZE, tok), f32),
            pltpu.VMEM((tok, heads * HEAD_SIZE), bf16),
        ]
        + [pltpu.VMEM(piece, bf16)] * 5
        + [pltpu.VMEM(piece, f32)] * 2
        + [dma((1 + 2 * local_kv,)), dma((chunks,))]
        + [dma((2, 2, local_kv))] * 4
        + [dma((2, chunks))] * 2
        + [dma((chunks,))] * 3,
        compiler_params=pltpu.CompilerParams(
            collective_id=0, has_side_effects=True, vmem_limit_bytes=60 * 1024 * 1024
        ),
    )(lengths, queries, keys, values, out_weight)
    return (mine + theirs.astype(f32)).astype(bf16)


def shifted(value, axis, steps):
    count = lax.axis_size(axis)
    first, last = (max(0, -steps), min(count, count - steps))
    return lax.ppermute(value, axis, [(source, source + steps) for source in range(first, last)])


def doc_of(positions, ends):
    return jnp.sum((positions[:, None] >= ends[None, :]).astype(jnp.int32), axis=1)


def shards(queries, keys, values, lengths, out_weight):
    tok = queries.shape[0]
    local_kv = keys.shape[1] // HEAD_SIZE
    query_group = queries.shape[1] // keys.shape[1]
    span = min(16, lax.axis_size("ctx") // 2)
    stretch = lax.axis_index("ctx")
    order = jnp.arange(lengths.shape[0])
    ends = jnp.sum(jnp.where(order[None, :] <= order[:, None], lengths[None, :], 0), axis=1)
    paired = jnp.stack([keys, values])
    window = paired
    have = 1
    while have < span + 1:
        count = min(have, span + 1 - have)
        received = shifted(window[:, window.shape[1] - count * tok :], "ctx", have)
        window = jnp.concatenate([received, window], axis=1)
        have = have + count
    blocks = jnp.swapaxes(window.reshape(2, span + 1, tok, local_kv * HEAD_SIZE), 0, 1)
    key_pos = (stretch - span) * tok + jnp.arange((span + 1) * tok, dtype=jnp.int32)
    key_pos = key_pos.reshape(span + 1, tok)
    query_pos = stretch * tok + jnp.arange(tok, dtype=jnp.int32)
    query_doc = doc_of(query_pos, ends)
    query_head_rows = queries.reshape(tok, local_kv, query_group, HEAD_SIZE)
    score_scale = 1.0 / HEAD_SIZE**0.5

    def step(carry, item):
        kv_block, positions = item
        allowed = (
            (doc_of(positions, ends)[None, :] == query_doc[:, None])
            & (positions[None, :] <= query_pos[:, None])
            & (positions[None, :] >= 0)
        )
        running, total, accum = carry
        key_head_rows = kv_block[0].reshape(tok, local_kv, HEAD_SIZE)
        value_heads = kv_block[1].reshape(tok, local_kv, HEAD_SIZE)
        logit_scores = (
            jnp.einsum(
                "hqnp,zqp->qnhz", query_head_rows, key_head_rows, preferred_element_type=jnp.float32
            )
            * score_scale
        )
        logit_scores = jnp.where(allowed, logit_scores, jnp.float32(-1e30))
        newest = jnp.maximum(running, jnp.max(logit_scores, axis=-1))
        factor = jnp.exp(running - newest)
        weights = jnp.where(allowed, jnp.exp(logit_scores - newest[..., None]), jnp.float32(0.0))
        total = total * factor + jnp.sum(weights, axis=-1)
        accum = accum * factor[..., None] + jnp.einsum(
            "wcju,uwn->wcjn",
            weights.astype(jnp.bfloat16),
            value_heads,
            preferred_element_type=jnp.float32,
        )
        result = (newest, total, accum)
        return (result, None)

    start_state = (
        jnp.full((local_kv, query_group, tok), -1e30, jnp.float32),
        jnp.zeros((local_kv, query_group, tok), jnp.float32),
        jnp.zeros((local_kv, query_group, tok, HEAD_SIZE), jnp.float32),
    )
    final_state, unused = lax.scan(step, start_state, (blocks, key_pos))
    attended = final_state[2] / final_state[1][..., None]
    attended = (
        jnp.transpose(attended, (2, 0, 1, 3))
        .reshape(tok, local_kv * query_group * HEAD_SIZE)
        .astype(jnp.bfloat16)
    )
    return lax.psum_scatter(
        jnp.dot(attended, out_weight, preferred_element_type=jnp.float32).astype(jnp.bfloat16),
        "head",
        scatter_dimension=0,
        tiled=True,
    )


def solution(mesh):
    in_specs = (P("ctx", "head"), P("ctx", "head"), P("ctx", "head"), P(), P("head", None))
    out_specs = P(("ctx", "head"), None)
    body = fused_shards if (mesh.shape["ctx"], mesh.shape["head"]) == (8, 4) else shards
    return jax.shard_map(body, mesh=mesh, in_specs=in_specs, out_specs=out_specs, check_vma=False)
```
